32 devices in a mesh: groups: 2 (over y), seq: 4 (over z), head: 4 (over x, core).
Axes of the slice: x: 2, y: 2, z: 4, core: 2. Of those that a mesh axis runs over, the one named last changes fastest.
Arguments:
- query: bfloat16 [8192, 1536], P(('groups', 'seq', 'head')), parts along dimension 0, may hold values from -150 to 150
- key_in: bfloat16 [8192, 1536], P(('groups', 'seq', 'head')), parts along dimension 0, may hold values from -6 to 6
- value: bfloat16 [8192, 1536], P(('groups', 'seq', 'head')), parts along dimension 0, may hold values from -6 to 6
- grad_out: bfloat16 [8192, 1536], P(('groups', 'seq', 'head')), parts along dimension 0, may hold values from -6 to 6
- pattern: int32 [16, 3], replicated, may hold values from 0 to 15, as said below
- live: int32 [16, 3], replicated, may hold values from 0 to 1, as said below
Outputs:
- attended: bfloat16 [8192, 1536], P(('groups', 'seq', 'head')), parts along dimension 0
- query_grad: bfloat16 [8192, 1536], P(('groups', 'seq', 'head')), parts along dimension 0
- key_grad: bfloat16 [8192, 1536], P(('groups', 'seq', 'head')), parts along dimension 0
- value_grad: bfloat16 [8192, 1536], P(('groups', 'seq', 'head')), parts along dimension 0
The draws below stay inside these ranges and needn't reach their ends.
There are 2 independent parts, one for each index of `groups`. The reference program is written for one: setup_inputs(seed, part) draws one part's arguments, and reference() takes and returns one part's arrays. A program takes and returns all parts, laid end to end along the dimension named above; an argument that names none is the same for every part. Nothing has to cross between parts.
Inputs may be any that keep to these rules, and one draw needn't show every extreme that they name: `pattern`: each entry names a tile of the same frame-tile layer as its query tile or of the layer just before or after it; the live entries of a row are distinct; an entry that is not live names the query tile itself. Slot 0 of every row is live and names the query tile itself.
All inputs are finite; a program needn't handle non-finite values.
Results may differ from the reference program's by a relative error of at most 0.015.
Values may be sent and summed in bfloat16 or wider, within the bound.
No kernel may reach another device: no remote copies, remote signals or barrier semaphores. Data moves between devices by JAX's collectives and lax.ppermute only.
A program may use at most 128 MiB of HBM per device.

```python
import jax
import jax.numpy as jnp
from jax import lax

HEADS = 12
HEAD_DIM = 128
TILE = 256
NB = 3
SPAN = 4
LAYERS = 4
NTILES = 16
TOKENS = 4096


def query_and_keys(key):
    shape = (TOKENS, HEADS * HEAD_DIM)
    keys = jax.random.truncated_normal(jax.random.fold_in(key, 101), -6.0, 6.0, shape, jnp.float32)
    queries = jax.random.truncated_normal(jax.random.fold_in(key, 102), -6.0, 6.0, shape, jnp.float32)
    return (queries, keys)


def draw_query(key, part):
    return query_and_keys(key)[0].astype(jnp.bfloat16)


def draw_key_in(key, part):
    return query_and_keys(key)[1].astype(jnp.bfloat16)


def neighbour_table(key):
    choices_count = 3 * SPAN
    tiles = jnp.arange(NTILES, dtype=jnp.int32)
    layer = tiles // SPAN
    spot = tiles % SPAN
    columns = jnp.arange(choices_count, dtype=jnp.int32)[None, :]
    noise = jax.random.randint(jax.random.fold_in(key, 201), (NTILES, choices_count), 0, 1 << 20)
    ranking = noise * choices_count + columns
    ranking = jnp.where(columns == (SPAN + spot)[:, None], jnp.int32(1 << 30), ranking)
    order = jnp.argsort(ranking, axis=1)[:, :NB - 1].astype(jnp.int32)
    target_layer = layer[:, None] + order // SPAN - 1
    target = target_layer * SPAN + order % SPAN
    inside = (target_layer >= 0) & (target_layer < LAYERS)
    keep = jax.random.randint(jax.random.fold_in(key, 202), (NTILES, NB - 1), 0, 4) > 0
    used = inside & keep
    table = jnp.concatenate([tiles[:, None], jnp.where(used, target, tiles[:, None])], axis=1).astype(jnp.int32)
    flags = jnp.concatenate([jnp.ones((NTILES, 1), jnp.int32), used.astype(jnp.int32)], axis=1)
    return (table, flags)


def draw_pattern(key, part):
    return neighbour_table(key)[0]


def draw_live(key, part):
    return neighbour_table(key)[1]


def block_scale(key, shape, pieces, least, top_value):
    factor_of = 1.0
    for dim, parts in pieces:
        draws = jax.random.uniform(jax.random.fold_in(jax.random.fold_in(key, 6), dim), (parts,), jnp.float32, least / len(pieces), top_value / len(pieces))
        factor_of = factor_of * jnp.repeat(jnp.exp(draws), shape[dim] // parts).reshape((-1,) + (1,) * (len(shape) - 1 - dim))
    return factor_of


def scatter_about(rng, shape, deviation, limit, shards=(), kind=jnp.bfloat16):
    gain = block_scale(rng, shape, shards, -0.22, 0.18) if shards else 1.0
    drawn = jax.random.normal(rng, shape, jnp.float32) * deviation * gain
    return jnp.minimum(jnp.maximum(drawn, -limit), limit).astype(kind)


def setup_inputs(seed: int = 0, part: int = 0) -> dict:
    key_of = jax.random.split(jax.random.key(seed), 7)
    own_keys = jax.random.split(jax.random.fold_in(key_of[6], part), 7)
    query = draw_query(jax.random.fold_in(jax.random.fold_in(key_of[6], part), 71), part)
    key_in = draw_key_in(jax.random.fold_in(jax.random.fold_in(key_of[6], part), 71), part)
    value = scatter_about(own_keys[2], (TOKENS, HEADS * HEAD_DIM), 1.0, 6.0, ((0, 16),))
    grad_out = scatter_about(own_keys[3], (TOKENS, HEADS * HEAD_DIM), 1.0, 6.0, ((0, 16),))
    pattern = draw_pattern(jax.random.fold_in(key_of[6], 71), part)
    live = draw_live(jax.random.fold_in(key_of[6], 71), part)
    return {"query": query, "key_in": key_in, "value": value, "grad_out": grad_out, "pattern": pattern, "live": live}


def reference(query, key_in, value, grad_out, pattern, live):
    width = HEADS * HEAD_DIM
    scale = HEAD_DIM ** -0.5
    queries = query.reshape(NTILES, TILE, HEADS, HEAD_DIM)
    keys = key_in.reshape(NTILES, TILE, HEADS, HEAD_DIM)
    values = value.reshape(NTILES, TILE, HEADS, HEAD_DIM)
    out_grads = grad_out.reshape(NTILES, TILE, HEADS, HEAD_DIM)

    def visit(carry, index):
        key_total, value_total = carry
        tile_ids = pattern[index].astype(jnp.int32)
        alive = live[index] > 0
        q_tile = queries[index].astype(jnp.float32)
        g_tile = out_grads[index].astype(jnp.float32)
        k_tiles = keys[tile_ids].astype(jnp.float32)
        v_tiles = values[tile_ids].astype(jnp.float32)
        scores = jnp.einsum('qhd,nkhd->hqnk', q_tile, k_tiles) * scale
        scores = jnp.where(alive[None, None, :, None], scores, -jnp.inf)
        peak = jnp.max(scores, axis=(2, 3), keepdims=True)
        exponent = jnp.exp(scores - peak)
        weights = exponent / jnp.sum(exponent, axis=(2, 3), keepdims=True)
        weights_low = lax.optimization_barrier(weights.astype(jnp.bfloat16)).astype(jnp.float32)
        attended = jnp.einsum('hqnk,nkhd->qhd', weights_low, v_tiles).astype(jnp.bfloat16)
        weight_grad = jnp.einsum('qhd,nkhd->hqnk', g_tile, v_tiles)
        delta = jnp.sum(weights * weight_grad, axis=(2, 3), keepdims=True)
        score_grad = lax.optimization_barrier((weights * (weight_grad - delta) * scale).astype(jnp.bfloat16)).astype(jnp.float32)
        query_grad = jnp.einsum('hqnk,nkhd->qhd', score_grad, k_tiles).astype(jnp.bfloat16)
        key_part = jnp.einsum('hqnk,qhd->nkhd', score_grad, q_tile)
        value_part = jnp.einsum('hqnk,qhd->nkhd', weights_low, g_tile)
        key_total = key_total.at[tile_ids].add(key_part)
        value_total = value_total.at[tile_ids].add(value_part)
        return (key_total, value_total), (attended, query_grad)

    zeros = jnp.zeros((NTILES, TILE, HEADS, HEAD_DIM), jnp.float32)
    (key_total, value_total), (attended, query_grad) = lax.scan(visit, (zeros, zeros), jnp.arange(NTILES, dtype=jnp.int32))
    return (attended.reshape(TOKENS, width), query_grad.reshape(TOKENS, width),
            key_total.astype(jnp.bfloat16).reshape(TOKENS, width), value_total.astype(jnp.bfloat16).reshape(TOKENS, width))
```

```python
import functools

import jax
import jax.numpy as jnp
from jax import lax
from jax.experimental import pallas as pl
from jax.experimental.pallas import tpu as pltpu
from jax.sharding import PartitionSpec as P

HEADS = 12
HEAD_DIM = 128
SLOTS = 3
SCALE = HEAD_DIM ** (-0.5)
BF = jnp.bfloat16
F32 = jnp.float32
PARAMS = pltpu.CompilerParams(vmem_limit_bytes=40 * 1024 * 1024)


def dot_nt(a, b):
    return lax.dot_general(a, b, (((1,), (1,)), ((), ())), preferred_element_type=F32)


def dot_nn(a, b):
    return lax.dot_general(a, b, (((1,), (0,)), ((), ())), preferred_element_type=F32)


def dot_tn(a, b):
    return lax.dot_general(a, b, (((0,), (0,)), ((), ())), preferred_element_type=F32)


def full(shape):
    return pl.BlockSpec(shape, lambda i, *_: (0,) * len(shape))


def cost(flops, nbytes):
    return pl.CostEstimate(flops=flops, bytes_accessed=nbytes, transcendentals=0)


class Plan:
    def __init__(self, members, tile):
        self.members = members
        self.tile = tile
        self.per = HEADS // members
        self.piece = (2, tile, HEAD_DIM)
        self.layer = (members, 2, tile, HEAD_DIM)

    def column(self, partner, chunk):
        per = self.per
        return pl.BlockSpec(
            (self.tile, HEAD_DIM), lambda i, pos: (0, (pos[1] ^ partner) * per + chunk)
        )


def pack(plan, pos, first, second):
    where = [(c, r) for c in range(plan.per) for r in range(1, plan.members)]
    count = len(where)

    def kernel(pos_ref, *refs):
        for n in range(count):
            refs[2 * count + n][0] = refs[2 * n][...]
            refs[2 * count + n][1] = refs[2 * n + 1][...]

    specs, operands = [], []
    for c, r in where:
        specs += [plan.column(r, c)] * 2
        operands += [first, second]
    out = pl.pallas_call(
        kernel,
        out_shape=[jax.ShapeDtypeStruct(plan.piece, BF)] * count,
        grid_spec=pltpu.PrefetchScalarGridSpec(
            num_scalar_prefetch=1,
            grid=(1,),
            in_specs=specs,
            out_specs=[full(plan.piece)] * count,
        ),
        compiler_params=PARAMS,
        cost_estimate=cost(0, 4 * count * plan.tile * HEAD_DIM * 2),
        name="pack",
    )(pos, *operands)
    return {key: out[n] for n, key in enumerate(where)}


def layer_of(plan, pos, chunk, key_in, value, pieces):
    def kernel(pos_ref, k_ref, v_ref, *refs):
        out = refs[-1]
        out[0, 0] = k_ref[...]
        out[0, 1] = v_ref[...]
        for r in range(1, plan.members):
            out[r] = refs[r - 1][...]

    return pl.pallas_call(
        kernel,
        out_shape=jax.ShapeDtypeStruct(plan.layer, BF),
        grid_spec=pltpu.PrefetchScalarGridSpec(
            num_scalar_prefetch=1,
            grid=(1,),
            in_specs=[plan.column(0, chunk)] * 2 + [full(plan.piece)] * (plan.members - 1),
            out_specs=full(plan.layer),
        ),
        compiler_params=PARAMS,
        cost_estimate=cost(0, 4 * plan.members * plan.tile * HEAD_DIM * 2),
        name="layer",
    )(pos, key_in, value, *pieces)


def attend(plan, pos, table, chunk, query, grad_out, qg, own, below, above):
    members, tile = plan.members, plan.tile

    def kernel(pos_ref, table_ref, q_ref, g_ref, *refs):
        qg_refs = refs[: members - 1]
        own_ref, below_ref, above_ref = refs[members - 1 : members + 2]
        odq_refs = refs[members + 2 : 2 * members + 2]
        down_ref, up_ref, sum_ref = refs[2 * members + 2 : 2 * members + 5]
        kv, qgs, odq, acc = refs[2 * members + 5 :]
        kv[pl.ds(0, members)] = below_ref[...]
        kv[pl.ds(members, members)] = own_ref[...]
        kv[pl.ds(2 * members, members)] = above_ref[...]
        qgs[0, 0] = q_ref[...]
        qgs[0, 1] = g_ref[...]
        for r in range(1, members):
            qgs[r] = qg_refs[r - 1][...]
        acc[...] = jnp.zeros_like(acc)
        seq, me = pos_ref[0], pos_ref[1]

        def place(tile_id):
            rel = tile_id - (seq - 1) * members
            return (rel // members) * members + ((rel % members) ^ me)

        def work(r, places):
            q, g = qgs[r, 0], qgs[r, 1]
            scores = [dot_nt(kv[p, 0], q) * SCALE for p in places]
            peak = functools.reduce(
                jnp.maximum, [jnp.max(s, axis=0, keepdims=True) for s in scores]
            )
            expo = [jnp.exp(s - peak) for s in scores]
            wgrad = [dot_nt(kv[p, 1], g) for p in places]
            total = sum(jnp.sum(e, axis=0, keepdims=True) for e in expo)
            mixed = sum(jnp.sum(e * w, axis=0, keepdims=True) for e, w in zip(expo, wgrad))
            inv = 1.0 / total
            delta = mixed * inv
            att_t, dq_t = 0.0, 0.0
            for p, e, w in zip(places, expo, wgrad):
                weight = e * inv
                low = weight.astype(BF)
                sgrad = (weight * (w - delta) * SCALE).astype(BF)
                att_t = att_t + dot_tn(kv[p, 1], low)
                dq_t = dq_t + dot_tn(kv[p, 0], sgrad)
                acc[p, 0] += dot_nn(sgrad, q)
                acc[p, 1] += dot_nn(low, g)
            odq[r, 0] = att_t.T.astype(BF)
            odq[r, 1] = dq_t.T.astype(BF)

        def step(r, carry):
            row = (seq * members + (r ^ me)) * 2 * SLOTS
            live = [table_ref[row + SLOTS + n] > 0 for n in range(SLOTS)]
            spots = [place(table_ref[row + n]) for n in range(SLOTS)]
            second = jnp.where(live[1], spots[1], spots[2])

            @pl.when(live[1] & live[2])
            def _():
                work(r, [spots[0], spots[1], spots[2]])

            @pl.when(live[1] ^ live[2])
            def _():
                work(r, [spots[0], second])

            @pl.when(jnp.logical_not(live[1] | live[2]))
            def _():
                work(r, [spots[0]])

            return carry

        lax.fori_loop(0, members, step, 0)
        for r in range(members):
            odq_refs[r][...] = odq[r]
        down_ref[...] = acc[pl.ds(0, members)].astype(BF)
        sum_ref[...] = acc[pl.ds(members, members)]
        up_ref[...] = acc[pl.ds(2 * members, members)].astype(BF)

    rows = members * tile * HEAD_DIM
    out = pl.pallas_call(
        kernel,
        out_shape=[jax.ShapeDtypeStruct(plan.piece, BF)] * members
        + [jax.ShapeDtypeStruct(plan.layer, BF)] * 2
        + [jax.ShapeDtypeStruct(plan.layer, F32)],
        grid_spec=pltpu.PrefetchScalarGridSpec(
            num_scalar_prefetch=2,
            grid=(1,),
            in_specs=[
                pl.BlockSpec((tile, HEAD_DIM), lambda i, p, t: (0, p[1] * plan.per + chunk))
            ]
            * 2
            + [full(plan.piece)] * (members - 1)
            + [full(plan.layer)] * 3,
            out_specs=[full(plan.piece)] * members + [full(plan.layer)] * 3,
            scratch_shapes=[
                pltpu.VMEM((3 * members, 2, tile, HEAD_DIM), BF),
                pltpu.VMEM(plan.layer, BF),
                pltpu.VMEM(plan.layer, BF),
                pltpu.VMEM((3 * members, 2, tile, HEAD_DIM), F32),
            ],
        ),
        compiler_params=PARAMS,
        cost_estimate=cost(12 * SLOTS * rows * tile * 2, 40 * rows),
        name="attend",
    )(pos, table, query, grad_out, *qg, own, below, above)
    return out[:members], out[members], out[members + 1], out[members + 2]


def owned(plan, total, from_above, from_below):
    members = plan.members

    def kernel(total_ref, above_ref, below_ref, *outs):
        for r in range(members):
            outs[r][...] = (
                total_ref[r] + above_ref[r].astype(F32) + below_ref[r].astype(F32)
            ).astype(BF)

    return pl.pallas_call(
        kernel,
        out_shape=[jax.ShapeDtypeStruct(plan.piece, BF)] * members,
        grid=(1,),
        in_specs=[full(plan.layer)] * 3,
        out_specs=[full(plan.piece)] * members,
        compiler_params=PARAMS,
        cost_estimate=cost(0, 20 * members * plan.tile * HEAD_DIM),
        name="owned",
    )(total, from_above, from_below)


def unpack(plan, pos, pieces):
    members, per = plan.members, plan.per
    where = [(c, r) for c in range(per) for r in range(members)]

    def kernel(pos_ref, *refs):
        first, second = refs[-2:]
        for n, (c, r) in enumerate(where):
            column = ((pos_ref[1] ^ r) * per + c) * HEAD_DIM
            span = pl.ds(pl.multiple_of(column, HEAD_DIM), HEAD_DIM)
            first[:, span] = refs[n][0]
            second[:, span] = refs[n][1]

    shape = (plan.tile, HEADS * HEAD_DIM)
    return pl.pallas_call(
        kernel,
        out_shape=[jax.ShapeDtypeStruct(shape, BF)] * 2,
        grid_spec=pltpu.PrefetchScalarGridSpec(
            num_scalar_prefetch=1,
            grid=(1,),
            in_specs=[full(plan.piece)] * len(where),
            out_specs=[full(shape)] * 2,
        ),
        compiler_params=PARAMS,
        cost_estimate=cost(0, 8 * plan.tile * HEADS * HEAD_DIM),
        name="unpack",
    )(pos, *[pieces[key] for key in where])


def swap(value, members, r):
    return lax.ppermute(value, "head", [(i, i ^ r) for i in range(members)])


def shifted(value, steps):
    count = lax.axis_size("seq")
    return lax.ppermute(
        value, "seq", [(i, i + steps) for i in range(count) if 0 <= i + steps < count]
    )


def body(query, key_in, value, grad_out, pattern, live):
    members = lax.axis_size("head")
    plan = Plan(members, query.shape[0])
    partners = range(1, members)
    chunks = range(plan.per)
    pos = jnp.stack([lax.axis_index("seq"), lax.axis_index("head")]).astype(jnp.int32)
    table = jnp.concatenate([pattern, live], axis=1).reshape(-1)

    kv_out = pack(plan, pos, key_in, value)
    qg_out = pack(plan, pos, query, grad_out)
    own, below, above, qg = {}, {}, {}, {}
    for c in chunks:
        got = [swap(kv_out[c, r], members, r) for r in partners]
        own[c] = layer_of(plan, pos, c, key_in, value, got)
        below[c] = shifted(own[c], 1)
        above[c] = shifted(own[c], -1)
        qg[c] = [swap(qg_out[c, r], members, r) for r in partners]
    odq, dkv = {}, {}
    for c in chunks:
        mine, down, up, total = attend(
            plan, pos, table, c, query, grad_out, qg[c], own[c], below[c], above[c]
        )
        odq[c, 0] = mine[0]
        for r in partners:
            odq[c, r] = swap(mine[r], members, r)
        sums = owned(plan, total, shifted(down, -1), shifted(up, 1))
        dkv[c, 0] = sums[0]
        for r in partners:
            dkv[c, r] = swap(sums[r], members, r)
    attended, query_grad = unpack(plan, pos, odq)
    key_grad, value_grad = unpack(plan, pos, dkv)
    return attended, query_grad, key_grad, value_grad


def solution(mesh):
    split = P(("groups", "seq", "head"), None)
    return jax.shard_map(
        body,
        mesh=mesh,
        in_specs=(split, split, split, split, P(), P()),
        out_specs=(split, split, split, split),
        check_vma=False,
    )
```

```python
import functools

import jax
import jax.numpy as jnp
from jax import lax
from jax.experimental import pallas as pl
from jax.experimental.pallas import tpu as pltpu
from jax.sharding import PartitionSpec as P

HEADS = 12
HEAD_DIM = 128
SLOTS = 3
SCALE = HEAD_DIM ** (-0.5)
BF = jnp.bfloat16
F32 = jnp.float32
MIB = 1024 * 1024
FULL = 60 * MIB
PARAMS = pltpu.CompilerParams(vmem_limit_bytes=20 * MIB)
ANYWHERE = pl.BlockSpec(memory_space=pl.ANY)
IN_HBM = pl.BlockSpec(memory_space=pltpu.HBM)


def dot_nt(a, b):
    return lax.dot_general(a, b, (((1,), (1,)), ((), ())), preferred_element_type=F32)


def dot_nn(a, b):
    return lax.dot_general(a, b, (((1,), (0,)), ((), ())), preferred_element_type=F32)


def dot_tn(a, b):
    return lax.dot_general(a, b, (((0,), (0,)), ((), ())), preferred_element_type=F32)


def full(shape):
    return pl.BlockSpec(shape, lambda i, *_: (0,) * len(shape))


def entry(index, *shape):
    return pl.BlockSpec((1,) + shape, lambda i, *_: (index,) + (0,) * len(shape))


def cost(flops, nbytes):
    return pl.CostEstimate(flops=flops, bytes_accessed=nbytes, transcendentals=0)


class Plan:
    def __init__(self, tile):
        self.tile = tile
        self.per = HEADS // 4
        self.piece = (2, tile, HEAD_DIM)
        self.layer = (4,) + self.piece


def move(plan, pos, inputs, shapes, moves, name, into=(), after=(), limit=2 * MIB):
    given, kept = len(inputs), len(into)
    extra = len(after)

    def kernel(pos_ref, *refs):
        sems = refs[-1]
        outs = refs[given + kept + extra : -1]

        def view(ref, where):
            if where[:1] == ("head",):
                column = ((pos_ref[1] ^ where[1]) * plan.per + where[2]) * HEAD_DIM
                return ref.at[:, pl.ds(pl.multiple_of(column, HEAD_DIM), HEAD_DIM)]
            return ref.at[where] if where else ref

        copies = [
            pltpu.make_async_copy(view(refs[a], u), view(outs[b], v), sems.at[n])
            for n, (a, u, b, v) in enumerate(moves)
        ]
        for copy in copies:
            copy.start()
        for copy in copies:
            copy.wait()

    specs = [IN_HBM if x.ndim == 2 else ANYWHERE for x in inputs] + [IN_HBM] * kept + [ANYWHERE] * extra
    return pl.pallas_call(
        kernel,
        out_shape=[jax.ShapeDtypeStruct(shape, BF) for shape in shapes],
        grid_spec=pltpu.PrefetchScalarGridSpec(
            num_scalar_prefetch=1,
            grid=(1,),
            in_specs=specs,
            out_specs=[IN_HBM if len(shape) == 2 else ANYWHERE for shape in shapes],
            scratch_shapes=[pltpu.SemaphoreType.DMA((len(moves),))],
        ),
        input_output_aliases={1 + given + n: n for n in range(kept)},
        compiler_params=pltpu.CompilerParams(vmem_limit_bytes=limit),
        cost_estimate=cost(0, 0),
        name=name,
    )(pos, *inputs, *into, *after)


def attend(plan, pos, table, chunk, query, grad_out, blocks):
    tile = plan.tile
    count = len(blocks)

    def kernel(pos_ref, table_ref, q_ref, g_ref, *refs):
        nears, fars = refs[:3], refs[3:6]
        qg_near, qg_far = refs[6:8]
        first, near, far, halo_a, halo_b, sum_ref = refs[count : count + 6]
        kv, qgs, odq, acc = refs[count + 6 :]
        for n in range(3):
            kv[pl.ds(4 * n, 2)] = nears[n][0]
            kv[pl.ds(4 * n + 2, 2)] = fars[n][0]
        qgs[0, 0] = q_ref[...]
        qgs[0, 1] = g_ref[...]
        qgs[1] = qg_near[0]
        qgs[pl.ds(2, 2)] = qg_far[0]
        acc[...] = jnp.zeros_like(acc)
        seq, me = pos_ref[0], pos_ref[1]

        def place(tile_id):
            rel = tile_id - (seq - 1) * 4
            turn = jnp.where((rel // 4 > 1) ^ (seq % 2 > 0), 1, 2)
            return jnp.where(rel // 4 == 1, 0, turn) * 4 + ((rel % 4) ^ me)

        def work(r, places):
            q, g = qgs[r, 0], qgs[r, 1]
            scores = [dot_nt(kv[p, 0], q) * SCALE for p in places]
            peak = functools.reduce(
                jnp.maximum, [jnp.max(s, axis=0, keepdims=True) for s in scores]
            )
            expo = [jnp.exp(s - peak) for s in scores]
            wgrad = [dot_nt(kv[p, 1], g) for p in places]
            total = sum(jnp.sum(e, axis=0, keepdims=True) for e in expo)
            mixed = sum(jnp.sum(e * w, axis=0, keepdims=True) for e, w in zip(expo, wgrad))
            inv = 1.0 / total
            delta = mixed * inv
            att_t, dq_t = 0.0, 0.0
            for p, e, w in zip(places, expo, wgrad):
                weight = e * inv
                low = weight.astype(BF)
                sgrad = (weight * (w - delta) * SCALE).astype(BF)
                att_t = att_t + dot_tn(kv[p, 1], low)
                dq_t = dq_t + dot_tn(kv[p, 0], sgrad)
                acc[p, 0] += dot_nn(sgrad, q)
                acc[p, 1] += dot_nn(low, g)
            odq[r, 0] = att_t.T.astype(BF)
            odq[r, 1] = dq_t.T.astype(BF)

        def step(r, carry):
            row = (seq * 4 + (r ^ me)) * 2 * SLOTS
            live = [table_ref[row + SLOTS + n] > 0 for n in range(SLOTS)]
            spots = [place(table_ref[row + n]) for n in range(SLOTS)]
            second = jnp.where(live[1], spots[1], spots[2])

            @pl.when(live[1] & live[2])
            def _():
                work(r, [spots[0], spots[1], spots[2]])

            @pl.when(live[1] ^ live[2])
            def _():
                work(r, [spots[0], second])

            @pl.when(jnp.logical_not(live[1] | live[2]))
            def _():
                work(r, [spots[0]])

            return carry

        lax.fori_loop(0, 4, step, 0)
        first[...] = odq[0]
        near[...] = odq[1]
        far[...] = odq[pl.ds(2, 2)]
        sum_ref[...] = acc[pl.ds(0, 4)]
        halo_a[...] = acc[pl.ds(4, 4)].astype(BF)
        halo_b[...] = acc[pl.ds(8, 4)].astype(BF)

    column = pl.BlockSpec((tile, HEAD_DIM), lambda i, p, t: (0, p[1] * plan.per + chunk))
    shapes = [plan.piece, plan.piece, (2,) + plan.piece, plan.layer, plan.layer]
    rows = 4 * tile * HEAD_DIM
    return pl.pallas_call(
        kernel,
        out_shape=[jax.ShapeDtypeStruct(shape, BF) for shape in shapes]
        + [jax.ShapeDtypeStruct(plan.layer, F32)],
        grid_spec=pltpu.PrefetchScalarGridSpec(
            num_scalar_prefetch=2,
            grid=(1,),
            in_specs=[column] * 2 + [spec for _, spec in blocks],
            out_specs=[full(shape) for shape in shapes + [plan.layer]],
            scratch_shapes=[
                pltpu.VMEM((12,) + plan.piece, BF),
                pltpu.VMEM(plan.layer, BF),
                pltpu.VMEM(plan.layer, BF),
                pltpu.VMEM((12,) + plan.piece, F32),
            ],
        ),
        compiler_params=PARAMS,
        cost_estimate=cost(60 * SLOTS * rows * tile, 40 * rows),
        name="attend",
    )(pos, table, query, grad_out, *[array for array, _ in blocks])


def owned(plan, pos, total, halos):
    def kernel(pos_ref, total_ref, halo_a, halo_b, first, near, far):
        for r in range(4):
            grads = total_ref[r]
            for n, halo in enumerate((halo_a, halo_b)):
                grads += jnp.where(pos_ref[2 + n] > 0, halo[r].astype(F32), 0.0)
            if r < 2:
                (first, near)[r][...] = grads.astype(BF)
            else:
                far[r - 2] = grads.astype(BF)

    shapes = [plan.piece, plan.piece, (2,) + plan.piece]
    return pl.pallas_call(
        kernel,
        out_shape=[jax.ShapeDtypeStruct(shape, BF) for shape in shapes],
        grid_spec=pltpu.PrefetchScalarGridSpec(
            num_scalar_prefetch=1,
            grid=(1,),
            in_specs=[full(plan.layer)] * 3,
            out_specs=[full(shape) for shape in shapes],
        ),
        compiler_params=PARAMS,
        cost_estimate=cost(0, 20 * 4 * plan.tile * HEAD_DIM),
        name="owned",
    )(pos, total, *halos)


def swap(value, r):
    return lax.ppermute(value, "head", [(i, i ^ r) for i in range(4)])


def exchange(value, turn):
    count = lax.axis_size("seq")
    pairs = []
    for s in range(count):
        other = s + 1 if s % 2 == turn else s - 1
        for h in range(4):
            there = other * 4 + h if 0 <= other < count else s * 4 + (h ^ 1)
            pairs.append((s * 4 + h, there))
    return lax.ppermute(value, ("seq", "head"), pairs)


def body(query, key_in, value, grad_out, pattern, live):
    plan = Plan(query.shape[0])
    per, piece = plan.per, plan.piece
    chunks = range(per)
    count = lax.axis_size("seq")
    seq = lax.axis_index("seq")
    met = []
    for turn in range(2):
        other = jnp.where(seq % 2 == turn, seq + 1, seq - 1)
        met.append((other >= 0) & (other < count))
    pos = jnp.stack([seq, lax.axis_index("head"), *met]).astype(jnp.int32)
    table = jnp.concatenate([pattern, live], axis=1).reshape(-1)

    def pick(r, c, out, *at):
        return [(a, ("head", r, c), out, at + (a,)) for a in range(2)]

    every, here, there = list(chunks), [key_in, value], [query, grad_out]

    def for_near(pair, name):
        moves = [m for n, r in enumerate((1, 3)) for c in every for m in pick(r, c, 0, n * per + c)]
        return swap(move(plan, pos, pair, [(2 * per,) + piece], moves, name)[0], 1)

    def for_far(pair, got, group, name, after=()):
        moves = []
        for n, c in enumerate(group):
            moves += pick(2, c, 0, n, 0)
            moves.append((2, (per + c,), 0, (n, 1)))
        shapes = [(len(group), 2) + piece]
        return move(plan, pos, [*pair, got], shapes, moves, name, after=after)[0]

    kv_got = for_near(here, "kv_for_near")
    qg_got = for_near(there, "qg_for_near")
    kv_parts, qg_parts = [every[:-1], every[-1:]], [every[:1], every[1:]]
    message = for_far(here, kv_got, kv_parts[0], "kv_for_far")
    far = [swap(message, 2)]
    moves = [m for c in every for m in pick(0, c, 0, c, 0)]
    moves += [(2, (c,), 0, (c, 1)) for c in every]
    near = move(plan, pos, [*here, kv_got], [(per, 2) + piece], moves, "kv_near", after=[message])[0]
    nears = [near] + [exchange(near, turn) for turn in range(2)]
    far.append(swap(for_far(here, kv_got, kv_parts[1], "kv_for_far", after=far[:1]), 2))
    fars = [[m] + [exchange(m, turn) for turn in range(2)] for m in far]
    qg_fars = [
        swap(for_far(there, qg_got, part, "qg_for_far", after=far[n : n + 1]), 2)
        for n, part in enumerate(qg_parts)
    ]

    odq, dkv = [], []
    for c in chunks:
        pair = (2,) + piece
        blocks = [(array, entry(c, *pair)) for array in nears]
        for arrays, parts in ((fars, kv_parts), ([[x] for x in qg_fars], qg_parts)):
            n = 0 if c in parts[0] else 1
            blocks += [(array, entry(c - parts[n][0], *pair)) for array in arrays[n]]
        blocks.insert(6, (qg_got, entry(c, *piece)))
        *mine, halo_a, halo_b, total = attend(plan, pos, table, c, query, grad_out, blocks)
        odq.append(mine[:2] + [swap(mine[2], 2)])
        halos = [exchange(halo, turn) for turn, halo in enumerate((halo_a, halo_b))]
        dkv.append(owned(plan, pos, total, halos))

    def onward(group, name, after=()):
        moves = []
        for c in range(len(group)):
            moves += [(2 * c, (), 0, (c, 0)), (2 * c + 1, (1,), 0, (c, 1))]
        inputs = [x for _, near, far in group for x in (near, far)]
        shapes = [(len(group), 2) + piece]
        return swap(move(plan, pos, inputs, shapes, moves, name, after=after)[0], 1)

    def columns(where):
        return [
            (a, view + (b,), b, ("head", r, c)) for a, view, r, c in where for b in range(2)
        ]

    shapes = [(plan.tile, HEADS * HEAD_DIM)] * 2

    def spread(group, got):
        inputs, where = [got], []
        for c, (first, _, far) in enumerate(group):
            where += [(0, (c, 0), 1, c), (0, (c, 1), 3, c)]
            where += [(len(inputs), (), 0, c), (len(inputs) + 1, (0,), 2, c)]
            inputs += [first, far]
        return inputs, where

    inputs, where = spread(odq, onward(odq, "odq_near", [dkv[-2][0]]))
    attended, query_grad = move(plan, pos, inputs, shapes, columns(where), "odq_out")

    early = [[first, near, swap(far, 2)] for first, near, far in dkv[:-1]]
    inputs, where = spread(early, onward(early, "dkv_near"))
    grads = move(plan, pos, inputs, shapes, columns(where), "dkv_early")
    first, near, far = dkv[-1]
    inputs = [first, swap(near, 1), swap(far[0], 2), swap(far[1], 3)]
    where = [(r, (), r, per - 1) for r in range(4)]
    key_grad, value_grad = move(plan, pos, inputs, shapes, columns(where), "dkv_out", into=grads)
    return attended, query_grad, key_grad, value_grad


def solution(mesh):
    split = P(("groups", "seq", "head"), None)
    return jax.shard_map(
        body,
        mesh=mesh,
        in_specs=(split, split, split, split, P(), P()),
        out_specs=(split, split, split, split),
        check_vma=False,
    )
```

```python
import functools

import jax
import jax.numpy as jnp
from jax import lax
from jax.experimental import pallas as pl
from jax.experimental.pallas import tpu as pltpu
from jax.sharding import PartitionSpec as P

HEADS = 12
HEAD_DIM = 128
SLOTS = 3
SCALE = HEAD_DIM ** (-0.5)
BF = jnp.bfloat16
F32 = jnp.float32
MIB = 1024 * 1024
TOKEN = (16, HEAD_DIM)
PARAMS = pltpu.CompilerParams(vmem_limit_bytes=20 * MIB)
ANYWHERE = pl.BlockSpec(memory_space=pl.ANY)


def dot_nt(a, b):
    return lax.dot_general(a, b, (((1,), (1,)), ((), ())), preferred_element_type=F32)


def dot_nn(a, b):
    return lax.dot_general(a, b, (((1,), (0,)), ((), ())), preferred_element_type=F32)


def dot_tn(a, b):
    return lax.dot_general(a, b, (((0,), (0,)), ((), ())), preferred_element_type=F32)


def full(shape):
    return pl.BlockSpec(shape, lambda i, *_: (0,) * len(shape))


def entry(index, *shape):
    return pl.BlockSpec((1,) + shape, lambda i, *_: (index,) + (0,) * len(shape))


def part(*index):
    return lambda i, *_: index + (0, 0, 0)


def cost(flops, nbytes):
    return pl.CostEstimate(flops=flops, bytes_accessed=nbytes, transcendentals=0)


class Plan:
    def __init__(self, tile):
        self.tile = tile
        self.per = HEADS // 4
        self.piece = (2, tile, HEAD_DIM)
        self.layer = (4,) + self.piece


def move(plan, pos, inputs, shapes, moves, name, into=(), after=()):
    given, kept = len(inputs), len(into)
    extra = len(after)

    def kernel(pos_ref, *refs):
        sems = refs[-1]
        outs = refs[given + kept + extra : -1]

        def view(ref, where):
            if where[:1] == ("head",):
                column = ((pos_ref[1] ^ where[1]) * plan.per + where[2]) * HEAD_DIM
                return ref.at[:, pl.ds(pl.multiple_of(column, HEAD_DIM), HEAD_DIM)]
            return ref.at[where] if where else ref

        copies = [
            pltpu.make_async_copy(view(refs[a], u), view(outs[b], v), sems.at[n])
            for n, (a, u, b, v) in enumerate(moves)
        ]
        for copy in copies:
            copy.start()
        for copy in copies:
            copy.wait()

    return pl.pallas_call(
        kernel,
        out_shape=[jax.ShapeDtypeStruct(shape, BF) for shape in shapes],
        grid_spec=pltpu.PrefetchScalarGridSpec(
            num_scalar_prefetch=1,
            grid=(1,),
            in_specs=[ANYWHERE] * (given + kept + extra),
            out_specs=[ANYWHERE] * len(shapes),
            scratch_shapes=[pltpu.SemaphoreType.DMA((len(moves),))],
        ),
        input_output_aliases={1 + given + n: n for n in range(kept)},
        compiler_params=pltpu.CompilerParams(vmem_limit_bytes=2 * MIB),
        cost_estimate=cost(0, 0),
        name=name,
    )(pos, *inputs, *into, *after)


def attend(plan, pos, table, chunk, query, grad_out, blocks, after=()):
    tile = plan.tile
    blocks = blocks + [(array, ANYWHERE) for array in after]
    count = len(blocks)

    def kernel(pos_ref, table_ref, q_ref, g_ref, *refs):
        nears, fars = refs[:3], refs[3:6]
        qg_near, qg_far = refs[6:8]
        first, near, far, halo_a, halo_b, sum_ref = refs[count : count + 6]
        kv, qgs, odq, acc = refs[count + 6 :]
        for n in range(3):
            kv[pl.ds(4 * n, 2)] = nears[n][0]
            kv[pl.ds(4 * n + 2, 2)] = fars[n][0]
        qgs[0, 0] = q_ref[...]
        qgs[0, 1] = g_ref[...]
        qgs[1] = qg_near[0]
        qgs[pl.ds(2, 2)] = qg_far[0]
        acc[...] = jnp.zeros_like(acc)
        seq, me = pos_ref[0], pos_ref[1]

        def place(tile_id):
            rel = tile_id - (seq - 1) * 4
            turn = jnp.where((rel // 4 > 1) ^ (seq % 2 > 0), 1, 2)
            return jnp.where(rel // 4 == 1, 0, turn) * 4 + ((rel % 4) ^ me)

        def work(r, places):
            q, g = qgs[r, 0], qgs[r, 1]
            scores = [dot_nt(kv[p, 0], q) * SCALE for p in places]
            peak = functools.reduce(
                jnp.maximum, [jnp.max(s, axis=0, keepdims=True) for s in scores]
            )
            expo = [jnp.exp(s - peak) for s in scores]
            wgrad = [dot_nt(kv[p, 1], g) for p in places]
            total = sum(jnp.sum(e, axis=0, keepdims=True) for e in expo)
            mixed = sum(jnp.sum(e * w, axis=0, keepdims=True) for e, w in zip(expo, wgrad))
            inv = 1.0 / total
            delta = mixed * inv
            att_t, dq_t = 0.0, 0.0
            for p, e, w in zip(places, expo, wgrad):
                weight = e * inv
                low = weight.astype(BF)
                sgrad = (weight * (w - delta) * SCALE).astype(BF)
                att_t = att_t + dot_tn(kv[p, 1], low)
                dq_t = dq_t + dot_tn(kv[p, 0], sgrad)
                acc[p, 0] += dot_nn(sgrad, q)
                acc[p, 1] += dot_nn(low, g)
            odq[r, 0] = att_t.T.astype(BF)
            odq[r, 1] = dq_t.T.astype(BF)

        def step(r, carry):
            row = (seq * 4 + (r ^ me)) * 2 * SLOTS
            live = [table_ref[row + SLOTS + n] > 0 for n in range(SLOTS)]
            spots = [place(table_ref[row + n]) for n in range(SLOTS)]
            second = jnp.where(live[1], spots[1], spots[2])

            @pl.when(live[1] & live[2])
            def _():
                work(r, [spots[0], spots[1], spots[2]])

            @pl.when(live[1] ^ live[2])
            def _():
                work(r, [spots[0], second])

            @pl.when(jnp.logical_not(live[1] | live[2]))
            def _():
                work(r, [spots[0]])

            return carry

        lax.fori_loop(0, 4, step, 0)
        first[...] = odq[0]
        near[...] = odq[1]
        far[...] = odq[pl.ds(2, 2)]
        sum_ref[...] = acc[pl.ds(0, 4)]
        halo_a[...] = acc[pl.ds(4, 4)].astype(BF)
        halo_b[...] = acc[pl.ds(8, 4)].astype(BF)

    column = pl.BlockSpec((tile, HEAD_DIM), lambda i, p, t: (0, p[1] * plan.per + chunk))
    shapes = [plan.piece, plan.piece, (2,) + plan.piece, plan.layer, plan.layer]
    rows = 4 * tile * HEAD_DIM
    return pl.pallas_call(
        kernel,
        out_shape=[jax.ShapeDtypeStruct(shape, BF) for shape in shapes]
        + [jax.ShapeDtypeStruct(plan.layer, F32)],
        grid_spec=pltpu.PrefetchScalarGridSpec(
            num_scalar_prefetch=2,
            grid=(1,),
            in_specs=[column] * 2 + [spec for _, spec in blocks],
            out_specs=[full(shape) for shape in shapes + [plan.layer]],
            scratch_shapes=[
                pltpu.VMEM((12,) + plan.piece, BF),
                pltpu.VMEM(plan.layer, BF),
                pltpu.VMEM(plan.layer, BF),
                pltpu.VMEM((12,) + plan.piece, F32),
            ],
        ),
        compiler_params=PARAMS,
        cost_estimate=cost(60 * SLOTS * rows * tile, 40 * rows),
        name="attend",
    )(pos, table, query, grad_out, *[array for array, _ in blocks])


def owned(plan, pos, total, halos, riders=(), after=()):
    count = len(riders)

    def kernel(pos_ref, total_ref, halo_a, halo_b, *refs):
        first, near, far = refs[-4:-1]
        for n in range(count):
            far[pl.ds(2 * n, 2)] = refs[n][...]
        for r in range(4):
            grads = total_ref[r]
            for n, halo in enumerate((halo_a, halo_b)):
                grads += jnp.where(pos_ref[2 + n] > 0, halo[r].astype(F32), 0.0)
            if r < 2:
                (first, near)[r][...] = grads.astype(BF)
            else:
                far[2 * count + r - 2] = grads.astype(BF)

    shapes = [plan.piece, plan.piece, (2 * count + 2,) + plan.piece]
    return pl.pallas_call(
        kernel,
        out_shape=[jax.ShapeDtypeStruct(shape, BF) for shape in shapes + [TOKEN]],
        grid_spec=pltpu.PrefetchScalarGridSpec(
            num_scalar_prefetch=1,
            grid=(1,),
            in_specs=[full(plan.layer)] * 3
            + [full((2,) + plan.piece)] * count
            + [ANYWHERE] * len(after),
            out_specs=[full(shape) for shape in shapes] + [ANYWHERE],
        ),
        compiler_params=PARAMS,
        cost_estimate=cost(0, 0),
        name="owned",
    )(pos, total, *halos, *riders, *after)


def swap(value, r):
    return lax.ppermute(value, "head", [(i, i ^ r) for i in range(4)])


def exchange(value, turn):
    count = lax.axis_size("seq")
    pairs = []
    for s in range(count):
        other = s + 1 if s % 2 == turn else s - 1
        for h in range(4):
            there = other * 4 + h if 0 <= other < count else s * 4 + (h ^ 1)
            pairs.append((s * 4 + h, there))
    return lax.ppermute(value, ("seq", "head"), pairs)


def body(query, key_in, value, grad_out, pattern, live):
    plan = Plan(query.shape[0])
    per, piece = plan.per, plan.piece
    chunks = range(per)
    count = lax.axis_size("seq")
    seq = lax.axis_index("seq")
    met = []
    for turn in range(2):
        other = jnp.where(seq % 2 == turn, seq + 1, seq - 1)
        met.append((other >= 0) & (other < count))
    pos = jnp.stack([seq, lax.axis_index("head"), *met]).astype(jnp.int32)
    table = jnp.concatenate([pattern, live], axis=1).reshape(-1)

    def pick(r, c, out, *at):
        return [(a, ("head", r, c), out, at + (a,)) for a in range(2)]

    every, here, there = list(chunks), [key_in, value], [query, grad_out]

    def for_near(pair, name):
        moves = [m for n, r in enumerate((1, 3)) for c in every for m in pick(r, c, 0, n * per + c)]
        return swap(move(plan, pos, pair, [(2 * per,) + piece], moves, name)[0], 1)

    def for_far(pair, got, group, name, after=()):
        moves = []
        for n, c in enumerate(group):
            moves += pick(2, c, 0, n, 0)
            moves.append((2, (per + c,), 0, (n, 1)))
        shapes = [(len(group), 2) + piece]
        return swap(move(plan, pos, [*pair, got], shapes, moves, name, after=after)[0], 2)

    kv_got = for_near(here, "kv_for_near")
    moves = [m for c in every for m in pick(0, c, 0, c, 0)]
    moves += [(2, (c,), 0, (c, 1)) for c in every]
    own = move(plan, pos, [*here, kv_got], [(per, 2) + piece], moves, "kv_near")[0]
    nears = [own] + [exchange(own, turn) for turn in range(2)]
    kv_parts, qg_parts = [every[:-1], every[-1:]], [every[:1], every[1:]]
    far = [for_far(here, kv_got, kv_parts[0], "kv_for_far", after=[own])]
    qg_got = for_near(there, "qg_for_near")
    qg_fars = [for_far(there, qg_got, qg_parts[0], "qg_for_far", after=far)]
    far.append(for_far(here, kv_got, kv_parts[1], "kv_for_far", after=far))
    qg_fars.append(for_far(there, qg_got, qg_parts[1], "qg_for_far", after=far[1:]))
    fars = [[m] + [exchange(m, turn) for turn in range(2)] for m in far]

    odq, sums = [], []
    for c in every:
        pair = (2,) + piece
        k, q = int(c not in kv_parts[0]), int(c not in qg_parts[0])
        blocks = [(array, entry(c, *pair)) for array in nears]
        blocks += [(array, entry(c - kv_parts[k][0], *pair)) for array in fars[k]]
        blocks += [(qg_got, entry(c, *piece)), (qg_fars[q], entry(c - qg_parts[q][0], *pair))]
        wait = [odq[0][2][0]] if c == every[-1] else []
        *mine, halo_a, halo_b, total = attend(
            plan, pos, table, c, query, grad_out, blocks, after=wait
        )
        if c < every[-1]:
            mine[2] = [swap(mine[2], 2), 0]
        odq.append(mine)
        halos = [exchange(halo, turn) for turn, halo in enumerate((halo_a, halo_b))]
        sums.append((total, halos))
    dkv, tokens = [], []
    for c in every:
        riders = [odq[-1][2]] if c == 0 else []
        wait = [odq[-2][2][0]] if c == 0 else []
        first, near, far, token = owned(plan, pos, *sums[c], riders, wait)
        if c < every[-1]:
            far = swap(far, 2)
        if c == 0:
            odq[-1][2] = [far, 0]
        dkv.append([first, near, [far, 2 * len(riders)]])
        tokens.append(token)

    def onward(group, name, after):
        moves, inputs = [], []
        for c, (_, near, (far, at)) in enumerate(group):
            moves += [(2 * c, (), 0, (c, 0)), (2 * c + 1, (at + 1,), 0, (c, 1))]
            inputs += [near, far]
        shapes = [(len(group), 2) + piece]
        return swap(move(plan, pos, inputs, shapes, moves, name, after=after)[0], 1)

    def columns(where):
        return [
            (a, view + (b,), b, ("head", r, c)) for a, view, r, c in where for b in range(2)
        ]

    shapes = [(plan.tile, HEADS * HEAD_DIM)] * 2

    def spread(group, got):
        inputs, where = [got], []
        for c, (first, _, (far, at)) in enumerate(group):
            where += [(0, (c, 0), 1, c), (0, (c, 1), 3, c)]
            where += [(len(inputs), (), 0, c), (len(inputs) + 1, (at,), 2, c)]
            inputs += [first, far]
        return inputs, where

    inputs, where = spread(odq, onward(odq, "odq_near", tokens[-2:-1]))
    attended, query_grad, token = move(plan, pos, inputs, shapes + [TOKEN], columns(where), "odq_out")

    inputs, where = spread(dkv[:-1], onward(dkv[:-1], "dkv_near", tokens[-1:]))
    grads = move(plan, pos, inputs, shapes, columns(where), "dkv_early")
    first, near, (far, _) = dkv[-1]
    inputs = [first, swap(near, 1), swap(far[0], 2), swap(far[1], 3)]
    where = [(r, (), r, per - 1) for r in range(4)]
    key_grad, value_grad = move(plan, pos, inputs, shapes, columns(where), "dkv_out", into=grads, after=[token])
    return attended, query_grad, key_grad, value_grad


def solution(mesh):
    split = P(("groups", "seq", "head"), None)
    return jax.shard_map(
        body,
        mesh=mesh,
        in_specs=(split, split, split, split, P(), P()),
        out_specs=(split, split, split, split),
        check_vma=False,
    )
```

```python
import functools

import jax
import jax.numpy as jnp
from jax import lax
from jax.experimental import pallas as pl
from jax.experimental.pallas import tpu as pltpu
from jax.sharding import PartitionSpec as P

HEADS = 12
HEAD_DIM = 128
SLOTS = 3
SCALE = HEAD_DIM ** (-0.5)
BF = jnp.bfloat16
F32 = jnp.float32
MIB = 1024 * 1024
TOKEN = (16, HEAD_DIM)
PARAMS = pltpu.CompilerParams(vmem_limit_bytes=20 * MIB)
ANYWHERE = pl.BlockSpec(memory_space=pl.ANY)


def dot_nt(a, b):
    return lax.dot_general(a, b, (((1,), (1,)), ((), ())), preferred_element_type=F32)


def dot_nn(a, b):
    return lax.dot_general(a, b, (((1,), (0,)), ((), ())), preferred_element_type=F32)


def dot_tn(a, b):
    return lax.dot_general(a, b, (((0,), (0,)), ((), ())), preferred_element_type=F32)


def full(shape):
    return pl.BlockSpec(shape, lambda i, *_: (0,) * len(shape))


def entry(index, *shape):
    return pl.BlockSpec((1,) + shape, lambda i, *_: (index,) + (0,) * len(shape))


def part(*index):
    return lambda i, *_: index + (0, 0, 0)


def cost(flops, nbytes):
    return pl.CostEstimate(flops=flops, bytes_accessed=nbytes, transcendentals=0)


class Plan:
    def __init__(self, tile):
        self.tile = tile
        self.per = HEADS // 4
        self.piece = (2, tile, HEAD_DIM)
        self.layer = (4,) + self.piece


def move(plan, pos, inputs, shapes, moves, name, into=(), after=()):
    given, kept = len(inputs), len(into)
    extra = len(after)

    def kernel(pos_ref, *refs):
        sems = refs[-1]
        outs = refs[given + kept + extra : -1]

        def view(ref, where):
            if where[:1] == ("head",):
                column = ((pos_ref[1] ^ where[1]) * plan.per + where[2]) * HEAD_DIM
                return ref.at[:, pl.ds(pl.multiple_of(column, HEAD_DIM), HEAD_DIM)]
            return ref.at[where] if where else ref

        copies = [
            pltpu.make_async_copy(view(refs[a], u), view(outs[b], v), sems.at[n])
            for n, (a, u, b, v) in enumerate(moves)
        ]
        for copy in copies:
            copy.start()
        for copy in copies:
            copy.wait()

    return pl.pallas_call(
        kernel,
        out_shape=[jax.ShapeDtypeStruct(shape, BF) for shape in shapes],
        grid_spec=pltpu.PrefetchScalarGridSpec(
            num_scalar_prefetch=1,
            grid=(1,),
            in_specs=[ANYWHERE] * (given + kept + extra),
            out_specs=[ANYWHERE] * len(shapes),
            scratch_shapes=[pltpu.SemaphoreType.DMA((len(moves),))],
        ),
        input_output_aliases={1 + given + n: n for n in range(kept)},
        compiler_params=pltpu.CompilerParams(vmem_limit_bytes=2 * MIB),
        cost_estimate=cost(0, 0),
        name=name,
    )(pos, *inputs, *into, *after)


def attend(plan, pos, table, chunk, query, grad_out, blocks, after=()):
    tile = plan.tile
    blocks = blocks + [(array, ANYWHERE) for array in after]
    count = len(blocks)

    def kernel(pos_ref, table_ref, q_ref, g_ref, *refs):
        nears, fars = refs[:3], refs[3:6]
        qg_near, qg_far = refs[6:8]
        first, near, far, halo_a, halo_b, sum_ref = refs[count : count + 6]
        kv, acc = refs[count + 6 :]
        for n in range(3):
            kv[pl.ds(4 * n, 2)] = nears[n][0]
            kv[pl.ds(4 * n + 2, 2)] = fars[n][0]
        acc[...] = jnp.zeros_like(acc)
        seq, me = pos_ref[0], pos_ref[1]

        def place(tile_id):
            rel = tile_id - (seq - 1) * 4
            turn = jnp.where((rel // 4 > 1) ^ (seq % 2 > 0), 1, 2)
            return jnp.where(rel // 4 == 1, 0, turn) * 4 + ((rel % 4) ^ me)

        def work(q, g, places, bias, out):
            scores = [dot_nt(kv[p, 0], q) * SCALE for p in places]
            scores = scores[:1] + [s + b for s, b in zip(scores[1:], bias)]
            peak = functools.reduce(
                jnp.maximum, [jnp.max(s, axis=0, keepdims=True) for s in scores]
            )
            expo = [jnp.exp(s - peak) for s in scores]
            wgrad = [dot_nt(kv[p, 1], g) for p in places]
            total = sum(jnp.sum(e, axis=0, keepdims=True) for e in expo)
            mixed = sum(jnp.sum(e * w, axis=0, keepdims=True) for e, w in zip(expo, wgrad))
            inv = 1.0 / total
            delta = mixed * inv
            att_t, dq_t = 0.0, 0.0
            for p, e, w in zip(places, expo, wgrad):
                weight = e * inv
                low = weight.astype(BF)
                sgrad = (weight * (w - delta) * SCALE).astype(BF)
                att_t = att_t + dot_tn(kv[p, 1], low)
                dq_t = dq_t + dot_tn(kv[p, 0], sgrad)
                acc[p, 0] += dot_nn(sgrad, q)
                acc[p, 1] += dot_nn(low, g)
            out[0] = att_t.T.astype(BF)
            out[1] = dq_t.T.astype(BF)

        tiles = [
            (q_ref[...], g_ref[...], first),
            (qg_near[0, 0], qg_near[0, 1], near),
            (qg_far[0, 0, 0], qg_far[0, 0, 1], far.at[0]),
            (qg_far[0, 1, 0], qg_far[0, 1, 1], far.at[1]),
        ]
        for r, (q, g, out) in enumerate(tiles):
            row = (seq * 4 + (r ^ me)) * 2 * SLOTS
            places = [r] + [place(table_ref[row + n]) for n in range(1, SLOTS)]
            bias = [
                jnp.where(table_ref[row + SLOTS + n] > 0, 0.0, -jnp.inf) for n in range(1, SLOTS)
            ]
            work(q, g, places, bias, out)
        sum_ref[...] = acc[pl.ds(0, 4)]
        halo_a[...] = acc[pl.ds(4, 4)].astype(BF)
        halo_b[...] = acc[pl.ds(8, 4)].astype(BF)

    column = pl.BlockSpec((tile, HEAD_DIM), lambda i, p, t: (0, p[1] * plan.per + chunk))
    shapes = [plan.piece, plan.piece, (2,) + plan.piece, plan.layer, plan.layer]
    rows = 4 * tile * HEAD_DIM
    return pl.pallas_call(
        kernel,
        out_shape=[jax.ShapeDtypeStruct(shape, BF) for shape in shapes]
        + [jax.ShapeDtypeStruct(plan.layer, F32)],
        grid_spec=pltpu.PrefetchScalarGridSpec(
            num_scalar_prefetch=2,
            grid=(1,),
            in_specs=[column] * 2 + [spec for _, spec in blocks],
            out_specs=[full(shape) for shape in shapes + [plan.layer]],
            scratch_shapes=[
                pltpu.VMEM((12,) + plan.piece, BF),
                pltpu.VMEM((12,) + plan.piece, F32),
            ],
        ),
        compiler_params=PARAMS,
        cost_estimate=cost(60 * SLOTS * rows * tile, 40 * rows),
        name="attend",
    )(pos, table, query, grad_out, *[array for array, _ in blocks])


def owned(plan, pos, total, halos, riders=(), after=()):
    count = len(riders)

    def kernel(pos_ref, total_ref, halo_a, halo_b, *refs):
        first, near, far = refs[-4:-1]
        for n in range(count):
            far[pl.ds(2 * n, 2)] = refs[n][...]
        for r in range(4):
            grads = total_ref[r]
            for n, halo in enumerate((halo_a, halo_b)):
                grads += jnp.where(pos_ref[2 + n] > 0, halo[r].astype(F32), 0.0)
            if r < 2:
                (first, near)[r][...] = grads.astype(BF)
            else:
                far[2 * count + r - 2] = grads.astype(BF)

    shapes = [plan.piece, plan.piece, (2 * count + 2,) + plan.piece]
    return pl.pallas_call(
        kernel,
        out_shape=[jax.ShapeDtypeStruct(shape, BF) for shape in shapes + [TOKEN]],
        grid_spec=pltpu.PrefetchScalarGridSpec(
            num_scalar_prefetch=1,
            grid=(1,),
            in_specs=[full(plan.layer)] * 3
            + [full((2,) + plan.piece)] * count
            + [ANYWHERE] * len(after),
            out_specs=[full(shape) for shape in shapes] + [ANYWHERE],
        ),
        compiler_params=PARAMS,
        cost_estimate=cost(0, 0),
        name="owned",
    )(pos, total, *halos, *riders, *after)


def swap(value, r):
    return lax.ppermute(value, "head", [(i, i ^ r) for i in range(4)])


def exchange(value, turn):
    count = lax.axis_size("seq")
    pairs = []
    for s in range(count):
        other = s + 1 if s % 2 == turn else s - 1
        for h in range(4):
            there = other * 4 + h if 0 <= other < count else s * 4 + (h ^ 1)
            pairs.append((s * 4 + h, there))
    return lax.ppermute(value, ("seq", "head"), pairs)


def body(query, key_in, value, grad_out, pattern, live):
    plan = Plan(query.shape[0])
    per, piece = plan.per, plan.piece
    chunks = range(per)
    count = lax.axis_size("seq")
    seq = lax.axis_index("seq")
    met = []
    for turn in range(2):
        other = jnp.where(seq % 2 == turn, seq + 1, seq - 1)
        met.append((other >= 0) & (other < count))
    pos = jnp.stack([seq, lax.axis_index("head"), *met]).astype(jnp.int32)
    table = jnp.concatenate([pattern, live], axis=1).reshape(-1)

    def pick(r, c, out, *at):
        return [(a, ("head", r, c), out, at + (a,)) for a in range(2)]

    every, here, there = list(chunks), [key_in, value], [query, grad_out]

    def for_near(pair, name):
        moves = [m for n, r in enumerate((1, 3)) for c in every for m in pick(r, c, 0, n * per + c)]
        return swap(move(plan, pos, pair, [(2 * per,) + piece], moves, name)[0], 1)

    def for_far(pair, got, group, name, after=()):
        moves = []
        for n, c in enumerate(group):
            moves += pick(2, c, 0, n, 0)
            moves.append((2, (per + c,), 0, (n, 1)))
        shapes = [(len(group), 2) + piece]
        return swap(move(plan, pos, [*pair, got], shapes, moves, name, after=after)[0], 2)

    kv_got = for_near(here, "kv_for_near")
    moves = [m for c in every for m in pick(0, c, 0, c, 0)]
    moves += [(2, (c,), 0, (c, 1)) for c in every]
    own = move(plan, pos, [*here, kv_got], [(per, 2) + piece], moves, "kv_near")[0]
    nears = [own] + [exchange(own, turn) for turn in range(2)]
    kv_parts, qg_parts = [every[:-1], every[-1:]], [every[:1], every[1:]]
    far = [for_far(here, kv_got, kv_parts[0], "kv_for_far", after=[own])]
    qg_got = for_near(there, "qg_for_near")
    qg_fars = [for_far(there, qg_got, qg_parts[0], "qg_for_far", after=far)]
    far.append(for_far(here, kv_got, kv_parts[1], "kv_for_far", after=far))
    qg_fars.append(for_far(there, qg_got, qg_parts[1], "qg_for_far", after=far[1:]))
    fars = [[m] + [exchange(m, turn) for turn in range(2)] for m in far]

    odq, sums = [], []
    for c in every:
        pair = (2,) + piece
        k, q = int(c not in kv_parts[0]), int(c not in qg_parts[0])
        blocks = [(array, entry(c, *pair)) for array in nears]
        blocks += [(array, entry(c - kv_parts[k][0], *pair)) for array in fars[k]]
        blocks += [(qg_got, entry(c, *piece)), (qg_fars[q], entry(c - qg_parts[q][0], *pair))]
        wait = [odq[0][2][0]] if c == every[-1] else []
        *mine, halo_a, halo_b, total = attend(
            plan, pos, table, c, query, grad_out, blocks, after=wait
        )
        if c < every[-1]:
            mine[2] = [swap(mine[2], 2), 0]
        odq.append(mine)
        halos = [exchange(halo, turn) for turn, halo in enumerate((halo_a, halo_b))]
        sums.append((total, halos))
    dkv, tokens = [], []
    for c in every:
        riders = [odq[-1][2]] if c == 0 else []
        wait = [odq[-2][2][0]] if c == 0 else []
        first, near, far, token = owned(plan, pos, *sums[c], riders, wait)
        if c < every[-1]:
            far = swap(far, 2)
        if c == 0:
            odq[-1][2] = [far, 0]
        dkv.append([first, near, [far, 2 * len(riders)]])
        tokens.append(token)

    def onward(group, name, after):
        moves, inputs = [], []
        for c, (_, near, (far, at)) in enumerate(group):
            moves += [(2 * c, (), 0, (c, 0)), (2 * c + 1, (at + 1,), 0, (c, 1))]
            inputs += [near, far]
        shapes = [(len(group), 2) + piece]
        return swap(move(plan, pos, inputs, shapes, moves, name, after=after)[0], 1)

    def columns(where):
        return [
            (a, view + (b,), b, ("head", r, c)) for a, view, r, c in where for b in range(2)
        ]

    shapes = [(plan.tile, HEADS * HEAD_DIM)] * 2

    def spread(group, got):
        inputs, where = [got], []
        for c, (first, _, (far, at)) in enumerate(group):
            where += [(0, (c, 0), 1, c), (0, (c, 1), 3, c)]
            where += [(len(inputs), (), 0, c), (len(inputs) + 1, (at,), 2, c)]
            inputs += [first, far]
        return inputs, where

    inputs, where = spread(odq, onward(odq, "odq_near", tokens[-2:-1]))
    attended, query_grad, token = move(plan, pos, inputs, shapes + [TOKEN], columns(where), "odq_out")

    inputs, where = spread(dkv[:-1], onward(dkv[:-1], "dkv_near", tokens[-1:]))
    grads = move(plan, pos, inputs, shapes, columns(where), "dkv_early")
    first, near, (far, _) = dkv[-1]
    inputs = [first, swap(near, 1), swap(far[0], 2), swap(far[1], 3)]
    where = [(r, (), r, per - 1) for r in range(4)]
    key_grad, value_grad = move(plan, pos, inputs, shapes, columns(where), "dkv_out", into=grads, after=[token])
    return attended, query_grad, key_grad, value_grad


def solution(mesh):
    split = P(("groups", "seq", "head"), None)
    return jax.shard_map(
        body,
        mesh=mesh,
        in_specs=(split, split, split, split, P(), P()),
        out_specs=(split, split, split, split),
        check_vma=False,
    )
```

```python
import functools

import jax
import jax.numpy as jnp
from jax import lax
from jax.experimental import pallas as pl
from jax.experimental.pallas import tpu as pltpu
from jax.sharding import PartitionSpec as P

HEADS = 12
HEAD_DIM = 128
SLOTS = 3
SCALE = HEAD_DIM ** (-0.5)
BF = jnp.bfloat16
F32 = jnp.float32
MIB = 1024 * 1024
TOKEN = (16, HEAD_DIM)
PARAMS = pltpu.CompilerParams(vmem_limit_bytes=20 * MIB)
ANYWHERE = pl.BlockSpec(memory_space=pl.ANY)


def dot_nt(a, b):
    return lax.dot_general(a, b, (((1,), (1,)), ((), ())), preferred_element_type=F32)


def dot_nn(a, b):
    return lax.dot_general(a, b, (((1,), (0,)), ((), ())), preferred_element_type=F32)


def dot_tn(a, b):
    return lax.dot_general(a, b, (((0,), (0,)), ((), ())), preferred_element_type=F32)


def full(shape):
    return pl.BlockSpec(shape, lambda i, *_: (0,) * len(shape))


def entry(index, *shape):
    return pl.BlockSpec((1,) + shape, lambda i, *_: (index,) + (0,) * len(shape))


def part(*index):
    return lambda i, *_: index + (0, 0, 0)


def cost(flops, nbytes):
    return pl.CostEstimate(flops=flops, bytes_accessed=nbytes, transcendentals=0)


class Plan:
    def __init__(self, tile):
        self.tile = tile
        self.per = HEADS // 4
        self.piece = (2, tile, HEAD_DIM)
        self.layer = (4,) + self.piece


def move(plan, pos, inputs, shapes, moves, name, into=(), after=()):
    given, kept = len(inputs), len(into)
    extra = len(after)

    def kernel(pos_ref, *refs):
        sems = refs[-1]
        outs = refs[given + kept + extra : -1]

        def view(ref, where):
            if where[:1] == ("head",):
                column = ((pos_ref[1] ^ where[1]) * plan.per + where[2]) * HEAD_DIM
                return ref.at[:, pl.ds(pl.multiple_of(column, HEAD_DIM), HEAD_DIM)]
            return ref.at[where] if where else ref

        copies = [
            pltpu.make_async_copy(view(refs[a], u), view(outs[b], v), sems.at[n])
            for n, (a, u, b, v) in enumerate(moves)
        ]
        for copy in copies:
            copy.start()
        for copy in copies:
            copy.wait()

    return pl.pallas_call(
        kernel,
        out_shape=[jax.ShapeDtypeStruct(shape, BF) for shape in shapes],
        grid_spec=pltpu.PrefetchScalarGridSpec(
            num_scalar_prefetch=1,
            grid=(1,),
            in_specs=[ANYWHERE] * (given + kept + extra),
            out_specs=[ANYWHERE] * len(shapes),
            scratch_shapes=[pltpu.SemaphoreType.DMA((len(moves),))],
        ),
        input_output_aliases={1 + given + n: n for n in range(kept)},
        compiler_params=pltpu.CompilerParams(vmem_limit_bytes=2 * MIB),
        cost_estimate=cost(0, 0),
        name=name,
    )(pos, *inputs, *into, *after)


def attend(plan, pos, table, chunk, query, grad_out, blocks, after=()):
    tile = plan.tile
    blocks = blocks + [(array, ANYWHERE) for array in after]
    count = len(blocks)

    def kernel(pos_ref, table_ref, q_ref, g_ref, *refs):
        nears, fars = refs[:3], refs[3:6]
        qg_near, qg_far = refs[6:8]
        first, near, far, halo_a, halo_b, sum_ref = refs[count : count + 6]
        kv, acc = refs[count + 6 :]
        for n in range(3):
            kv[pl.ds(4 * n, 2)] = nears[n][0]
            kv[pl.ds(4 * n + 2, 2)] = fars[n][0]
        acc[...] = jnp.zeros_like(acc)
        seq, me = pos_ref[0], pos_ref[1]

        def place(tile_id):
            rel = tile_id - (seq - 1) * 4
            turn = jnp.where((rel // 4 > 1) ^ (seq % 2 > 0), 1, 2)
            return jnp.where(rel // 4 == 1, 0, turn) * 4 + ((rel % 4) ^ me)

        def work(q, g, places, bias, out):
            scores = [dot_nt(kv[p, 0], q) * SCALE for p in places]
            scores = scores[:1] + [s + b for s, b in zip(scores[1:], bias)]
            peak = functools.reduce(
                jnp.maximum, [jnp.max(s, axis=0, keepdims=True) for s in scores]
            )
            expo = [jnp.exp(s - peak) for s in scores]
            wgrad = [dot_nt(kv[p, 1], g) for p in places]
            total = sum(jnp.sum(e, axis=0, keepdims=True) for e in expo)
            mixed = sum(jnp.sum(e * w, axis=0, keepdims=True) for e, w in zip(expo, wgrad))
            inv = 1.0 / total
            delta = mixed * inv
            att_t, dq_t = 0.0, 0.0
            for p, e, w in zip(places, expo, wgrad):
                weight = e * inv
                low = weight.astype(BF)
                sgrad = (weight * (w - delta) * SCALE).astype(BF)
                att_t = att_t + dot_tn(kv[p, 1], low)
                dq_t = dq_t + dot_tn(kv[p, 0], sgrad)
                acc[p, 0] += dot_nn(sgrad, q)
                acc[p, 1] += dot_nn(low, g)
            out[0] = att_t.T.astype(BF)
            out[1] = dq_t.T.astype(BF)

        tiles = [
            (q_ref[...], g_ref[...], first),
            (qg_near[0, 0], qg_near[0, 1], near),
            (qg_far[0, 0, 0], qg_far[0, 0, 1], far.at[0]),
            (qg_far[0, 1, 0], qg_far[0, 1, 1], far.at[1]),
        ]
        for r, (q, g, out) in enumerate(tiles):
            row = (seq * 4 + (r ^ me)) * 2 * SLOTS
            places = [r] + [place(table_ref[row + n]) for n in range(1, SLOTS)]
            bias = [
                jnp.where(table_ref[row + SLOTS + n] > 0, 0.0, -jnp.inf) for n in range(1, SLOTS)
            ]
            work(q, g, places, bias, out)
        sum_ref[...] = acc[pl.ds(0, 4)]
        halo_a[...] = acc[pl.ds(4, 4)].astype(BF)
        halo_b[...] = acc[pl.ds(8, 4)].astype(BF)

    column = pl.BlockSpec((tile, HEAD_DIM), lambda i, p, t: (0, p[1] * plan.per + chunk))
    shapes = [plan.piece, plan.piece, (2,) + plan.piece, plan.layer, plan.layer]
    rows = 4 * tile * HEAD_DIM
    return pl.pallas_call(
        kernel,
        out_shape=[jax.ShapeDtypeStruct(shape, BF) for shape in shapes]
        + [jax.ShapeDtypeStruct(plan.layer, F32)],
        grid_spec=pltpu.PrefetchScalarGridSpec(
            num_scalar_prefetch=2,
            grid=(1,),
            in_specs=[column] * 2 + [spec for _, spec in blocks],
            out_specs=[full(shape) for shape in shapes + [plan.layer]],
            scratch_shapes=[
                pltpu.VMEM((12,) + plan.piece, BF),
                pltpu.VMEM((12,) + plan.piece, F32),
            ],
        ),
        compiler_params=PARAMS,
        cost_estimate=cost(60 * SLOTS * rows * tile, 40 * rows),
        name="attend",
    )(pos, table, query, grad_out, *[array for array, _ in blocks])


def owned(plan, pos, total, halos, riders=(), beside=(), after=()):
    count, extra = len(riders), len(beside)

    def kernel(pos_ref, total_ref, halo_a, halo_b, *refs):
        first, near, far = refs[-4:-1]
        for n in range(count):
            far[pl.ds(2 * n, 2)] = refs[n][...]
        for n in range(extra):
            near[n] = refs[count + n][...]
        for r in range(4):
            grads = total_ref[r]
            for n, halo in enumerate((halo_a, halo_b)):
                grads += jnp.where(pos_ref[2 + n] > 0, halo[r].astype(F32), 0.0)
            if r == 0:
                first[...] = grads.astype(BF)
            elif r == 1:
                near[extra] = grads.astype(BF)
            else:
                far[2 * count + r - 2] = grads.astype(BF)

    shapes = [plan.piece, (extra + 1,) + plan.piece, (2 * count + 2,) + plan.piece]
    return pl.pallas_call(
        kernel,
        out_shape=[jax.ShapeDtypeStruct(shape, BF) for shape in shapes + [TOKEN]],
        grid_spec=pltpu.PrefetchScalarGridSpec(
            num_scalar_prefetch=1,
            grid=(1,),
            in_specs=[full(plan.layer)] * 3
            + [full((2,) + plan.piece)] * count
            + [full(plan.piece)] * extra
            + [ANYWHERE] * len(after),
            out_specs=[full(shape) for shape in shapes] + [ANYWHERE],
        ),
        compiler_params=PARAMS,
        cost_estimate=cost(0, 0),
        name="owned",
    )(pos, total, *halos, *riders, *beside, *after)


def swap(value, r):
    return lax.ppermute(value, "head", [(i, i ^ r) for i in range(4)])


def exchange(value, turn):
    count = lax.axis_size("seq")
    pairs = []
    for s in range(count):
        other = s + 1 if s % 2 == turn else s - 1
        for h in range(4):
            there = other * 4 + h if 0 <= other < count else s * 4 + (h ^ 1)
            pairs.append((s * 4 + h, there))
    return lax.ppermute(value, ("seq", "head"), pairs)


def body(query, key_in, value, grad_out, pattern, live):
    plan = Plan(query.shape[0])
    per, piece = plan.per, plan.piece
    chunks = range(per)
    count = lax.axis_size("seq")
    seq = lax.axis_index("seq")
    met = []
    for turn in range(2):
        other = jnp.where(seq % 2 == turn, seq + 1, seq - 1)
        met.append((other >= 0) & (other < count))
    pos = jnp.stack([seq, lax.axis_index("head"), *met]).astype(jnp.int32)
    table = jnp.concatenate([pattern, live], axis=1).reshape(-1)

    def pick(r, c, out, *at):
        return [(a, ("head", r, c), out, at + (a,)) for a in range(2)]

    every, here, there = list(chunks), [key_in, value], [query, grad_out]

    def for_near(pair, name):
        moves = [m for n, r in enumerate((1, 3)) for c in every for m in pick(r, c, 0, n * per + c)]
        return swap(move(plan, pos, pair, [(2 * per,) + piece], moves, name)[0], 1)

    def for_far(pair, got, group, name, after=()):
        moves = []
        for n, c in enumerate(group):
            moves += pick(2, c, 0, n, 0)
            moves.append((2, (per + c,), 0, (n, 1)))
        shapes = [(len(group), 2) + piece]
        return swap(move(plan, pos, [*pair, got], shapes, moves, name, after=after)[0], 2)

    kv_got = for_near(here, "kv_for_near")
    moves = [m for c in every for m in pick(0, c, 0, c, 0)]
    moves += [(2, (c,), 0, (c, 1)) for c in every]
    own = move(plan, pos, [*here, kv_got], [(per, 2) + piece], moves, "kv_near")[0]
    nears = [own] + [exchange(own, turn) for turn in range(2)]
    kv_parts, qg_parts = [every[:-1], every[-1:]], [every[:1], every[1:]]
    far = [for_far(here, kv_got, kv_parts[0], "kv_for_far", after=[own])]
    qg_got = for_near(there, "qg_for_near")
    qg_fars = [for_far(there, qg_got, qg_parts[0], "qg_for_far", after=far)]
    far.append(for_far(here, kv_got, kv_parts[1], "kv_for_far", after=far))
    qg_fars.append(for_far(there, qg_got, qg_parts[1], "qg_for_far", after=far[1:]))
    fars = [[m] + [exchange(m, turn) for turn in range(2)] for m in far]

    odq, sums = [], []
    for c in every:
        pair = (2,) + piece
        k, q = int(c not in kv_parts[0]), int(c not in qg_parts[0])
        blocks = [(array, entry(c, *pair)) for array in nears]
        blocks += [(array, entry(c - kv_parts[k][0], *pair)) for array in fars[k]]
        blocks += [(qg_got, entry(c, *piece)), (qg_fars[q], entry(c - qg_parts[q][0], *pair))]
        wait = [odq[0][2][0]] if c == every[-1] else []
        *mine, halo_a, halo_b, total = attend(
            plan, pos, table, c, query, grad_out, blocks, after=wait
        )
        if c < every[-1]:
            mine[2] = [swap(mine[2], 2), 0]
        odq.append(mine)
        halos = [exchange(halo, turn) for turn, halo in enumerate((halo_a, halo_b))]
        sums.append((total, halos))
    dkv, tokens = [], []
    for c in every:
        riders = [odq[-1][2]] if c == 0 else []
        wait = [odq[-2][2][0]] if c == 0 else []
        beside = [dkv[-1][1][0]] if c == every[-1] else []
        first, near, far, token = owned(plan, pos, *sums[c], riders, beside, wait)
        if c < every[-1]:
            far = swap(far, 2)
        if c == 0:
            odq[-1][2] = [far, 0]
        dkv.append([first, near, [far, 2 * len(riders)]])
        tokens.append(token)

    def onward(groups, name, after):
        moves, inputs = [], []
        for n, group in enumerate(groups):
            for c, (_, near, (far, at)) in enumerate(group):
                view = (0,) if near.ndim > len(piece) else ()
                moves += [(len(inputs), view, n, (c, 0)), (len(inputs) + 1, (at + 1,), n, (c, 1))]
                inputs += [near, far]
        shapes = [(len(group), 2) + piece for group in groups]
        return [swap(x, 1) for x in move(plan, pos, inputs, shapes, moves, name, after=after)]

    got = onward([odq[:-1]], "odq_near", [])
    got += onward([odq[-1:], dkv[:1]], "late_near", tokens[1:2])

    shapes = [(plan.tile, HEADS * HEAD_DIM)] * 4
    inputs, moves = list(got), []
    for n, (first, _, (far, at)) in enumerate(odq + dkv[:1]):
        m, c = divmod(n, per)
        source, at_c = (0, n) if n < per - 1 else (n - per + 2, 0)
        pieces = [(len(inputs), ()), (source, (at_c, 0)), (len(inputs) + 1, (at,)), (source, (at_c, 1))]
        for r, (a, view) in enumerate(pieces):
            moves += [(a, view + (b,), 2 * m + b, ("head", r, c)) for b in range(2)]
        inputs += [first, far]
    attended, query_grad, *grads = move(plan, pos, inputs, shapes, moves, "outputs")

    (first_1, _, (far_1, at)), (first_2, near_2, (far_2, _)) = dkv[1:]
    beside = swap(near_2, 1)
    inputs = [first_1, beside, far_1, swap(far_1[at + 1], 1)]
    inputs += [first_2, swap(far_2[0], 2), swap(far_2[1], 3)]
    where = [(0, (), 0, 1), (1, (0,), 1, 1), (2, (at,), 2, 1), (3, (), 3, 1)]
    where += [(4, (), 0, 2), (1, (1,), 1, 2), (5, (), 2, 2), (6, (), 3, 2)]
    moves = [(a, view + (b,), b, ("head", r, c)) for a, view, r, c in where for b in range(2)]
    key_grad, value_grad = move(plan, pos, inputs, shapes[:2], moves, "last", into=grads)
    return attended, query_grad, key_grad, value_grad


def solution(mesh):
    split = P(("groups", "seq", "head"), None)
    return jax.shard_map(
        body,
        mesh=mesh,
        in_specs=(split, split, split, split, P(), P()),
        out_specs=(split, split, split, split),
        check_vma=False,
    )
```

```python
import functools

import jax
import jax.numpy as jnp
from jax import lax
from jax.experimental import pallas as pl
from jax.experimental.pallas import tpu as pltpu
from jax.sharding import PartitionSpec as P

HEADS = 12
HEAD_DIM = 128
SLOTS = 3
SCALE = HEAD_DIM ** (-0.5)
BF = jnp.bfloat16
F32 = jnp.float32
MIB = 1024 * 1024
TOKEN = (16, HEAD_DIM)
PARAMS = pltpu.CompilerParams(vmem_limit_bytes=20 * MIB)
ANYWHERE = pl.BlockSpec(memory_space=pl.ANY)


def dot_nt(a, b):
    return lax.dot_general(a, b, (((1,), (1,)), ((), ())), preferred_element_type=F32)


def dot_nn(a, b):
    return lax.dot_general(a, b, (((1,), (0,)), ((), ())), preferred_element_type=F32)


def dot_tn(a, b):
    return lax.dot_general(a, b, (((0,), (0,)), ((), ())), preferred_element_type=F32)


def full(shape):
    return pl.BlockSpec(shape, lambda i, *_: (0,) * len(shape))


def entry(index, *shape):
    return pl.BlockSpec((1,) + shape, lambda i, *_: (index,) + (0,) * len(shape))


def part(*index):
    return lambda i, *_: index + (0, 0, 0)


def cost(flops, nbytes):
    return pl.CostEstimate(flops=flops, bytes_accessed=nbytes, transcendentals=0)


class Plan:
    def __init__(self, tile):
        self.tile = tile
        self.per = HEADS // 4
        self.piece = (2, tile, HEAD_DIM)
        self.layer = (4,) + self.piece


def move(plan, pos, inputs, shapes, moves, name, into=(), after=()):
    given, kept = len(inputs), len(into)
    extra = len(after)

    def kernel(pos_ref, *refs):
        sems = refs[-1]
        outs = refs[given + kept + extra : -1]

        def view(ref, where):
            if where[:1] == ("head",):
                column = ((pos_ref[1] ^ where[1]) * plan.per + where[2]) * HEAD_DIM
                return ref.at[:, pl.ds(pl.multiple_of(column, HEAD_DIM), HEAD_DIM)]
            return ref.at[where] if where else ref

        copies = [
            pltpu.make_async_copy(view(refs[a], u), view(outs[b], v), sems.at[n])
            for n, (a, u, b, v) in enumerate(moves)
        ]
        for copy in copies:
            copy.start()
        for copy in copies:
            copy.wait()

    return pl.pallas_call(
        kernel,
        out_shape=[jax.ShapeDtypeStruct(shape, BF) for shape in shapes],
        grid_spec=pltpu.PrefetchScalarGridSpec(
            num_scalar_prefetch=1,
            grid=(1,),
            in_specs=[ANYWHERE] * (given + kept + extra),
            out_specs=[ANYWHERE] * len(shapes),
            scratch_shapes=[pltpu.SemaphoreType.DMA((len(moves),))],
        ),
        input_output_aliases={1 + given + n: n for n in range(kept)},
        compiler_params=pltpu.CompilerParams(vmem_limit_bytes=2 * MIB),
        cost_estimate=cost(0, 0),
        name=name,
    )(pos, *inputs, *into, *after)


def attend(plan, pos, table, chunk, query, grad_out, blocks, after=()):
    tile = plan.tile
    blocks = blocks + [(array, ANYWHERE) for array in after]
    count = len(blocks)

    def kernel(pos_ref, table_ref, q_ref, g_ref, *refs):
        nears, fars = refs[:3], refs[3:6]
        qg_near, qg_far = refs[6:8]
        first, near, far, halo_a, halo_b, sum_ref = refs[count : count + 6]
        kv, acc = refs[count + 6 :]
        for n in range(3):
            kv[pl.ds(4 * n, 2)] = nears[n][0]
            kv[pl.ds(4 * n + 2, 2)] = fars[n][0]
        acc[...] = jnp.zeros_like(acc)
        seq, me = pos_ref[0], pos_ref[1]

        def place(tile_id):
            rel = tile_id - (seq - 1) * 4
            turn = jnp.where((rel // 4 > 1) ^ (seq % 2 > 0), 1, 2)
            return jnp.where(rel // 4 == 1, 0, turn) * 4 + ((rel % 4) ^ me)

        def work(q, g, places, bias, out):
            scores = [dot_nt(kv[p, 0], q) * SCALE for p in places]
            scores = scores[:1] + [s + b for s, b in zip(scores[1:], bias)]
            peak = functools.reduce(
                jnp.maximum, [jnp.max(s, axis=0, keepdims=True) for s in scores]
            )
            expo = [jnp.exp(s - peak) for s in scores]
            wgrad = [dot_nt(kv[p, 1], g) for p in places]
            total = sum(jnp.sum(e, axis=0, keepdims=True) for e in expo)
            mixed = sum(jnp.sum(e * w, axis=0, keepdims=True) for e, w in zip(expo, wgrad))
            inv = 1.0 / total
            delta = mixed * inv
            att_t, dq_t = 0.0, 0.0
            for p, e, w in zip(places, expo, wgrad):
                weight = e * inv
                low = weight.astype(BF)
                sgrad = (weight * (w - delta) * SCALE).astype(BF)
                att_t = att_t + dot_tn(kv[p, 1], low)
                dq_t = dq_t + dot_tn(kv[p, 0], sgrad)
                acc[p, 0] += dot_nn(sgrad, q)
                acc[p, 1] += dot_nn(low, g)
            out[0] = att_t.T.astype(BF)
            out[1] = dq_t.T.astype(BF)

        tiles = [
            (q_ref[...], g_ref[...], first),
            (qg_near[0, 0], qg_near[0, 1], near),
            (qg_far[0, 0, 0], qg_far[0, 0, 1], far.at[0]),
            (qg_far[0, 1, 0], qg_far[0, 1, 1], far.at[1]),
        ]
        for r, (q, g, out) in enumerate(tiles):
            row = (seq * 4 + (r ^ me)) * 2 * SLOTS
            places = [r] + [place(table_ref[row + n]) for n in range(1, SLOTS)]
            bias = [
                jnp.where(table_ref[row + SLOTS + n] > 0, 0.0, -jnp.inf) for n in range(1, SLOTS)
            ]
            work(q, g, places, bias, out)
        sum_ref[...] = acc[pl.ds(0, 4)]
        halo_a[...] = acc[pl.ds(4, 4)].astype(BF)
        halo_b[...] = acc[pl.ds(8, 4)].astype(BF)

    column = pl.BlockSpec((tile, HEAD_DIM), lambda i, p, t: (0, p[1] * plan.per + chunk))
    shapes = [plan.piece, plan.piece, (2,) + plan.piece, plan.layer, plan.layer]
    rows = 4 * tile * HEAD_DIM
    return pl.pallas_call(
        kernel,
        out_shape=[jax.ShapeDtypeStruct(shape, BF) for shape in shapes]
        + [jax.ShapeDtypeStruct(plan.layer, F32)],
        grid_spec=pltpu.PrefetchScalarGridSpec(
            num_scalar_prefetch=2,
            grid=(1,),
            in_specs=[column] * 2 + [spec for _, spec in blocks],
            out_specs=[full(shape) for shape in shapes + [plan.layer]],
            scratch_shapes=[
                pltpu.VMEM((12,) + plan.piece, BF),
                pltpu.VMEM((12,) + plan.piece, F32),
            ],
        ),
        compiler_params=PARAMS,
        cost_estimate=cost(60 * SLOTS * rows * tile, 40 * rows),
        name="attend",
    )(pos, table, query, grad_out, *[array for array, _ in blocks])


def owned(plan, pos, total, halos, riders=(), beside=(), after=()):
    count, extra = len(riders), len(beside)

    def kernel(pos_ref, total_ref, halo_a, halo_b, *refs):
        first, near, far = refs[-4:-1]
        for n in range(count):
            far[pl.ds(2 * n, 2)] = refs[n][...]
        for n in range(extra):
            near[n] = refs[count + n][...]
        for r in range(4):
            grads = total_ref[r]
            for n, halo in enumerate((halo_a, halo_b)):
                grads += jnp.where(pos_ref[2 + n] > 0, halo[r].astype(F32), 0.0)
            if r == 0:
                first[...] = grads.astype(BF)
            elif r == 1:
                near[extra] = grads.astype(BF)
            else:
                far[2 * count + r - 2] = grads.astype(BF)

    shapes = [plan.piece, (extra + 1,) + plan.piece, (2 * count + 2,) + plan.piece]
    return pl.pallas_call(
        kernel,
        out_shape=[jax.ShapeDtypeStruct(shape, BF) for shape in shapes + [TOKEN]],
        grid_spec=pltpu.PrefetchScalarGridSpec(
            num_scalar_prefetch=1,
            grid=(1,),
            in_specs=[full(plan.layer)] * 3
            + [full((2,) + plan.piece)] * count
            + [full(plan.piece)] * extra
            + [ANYWHERE] * len(after),
            out_specs=[full(shape) for shape in shapes] + [ANYWHERE],
        ),
        compiler_params=PARAMS,
        cost_estimate=cost(0, 0),
        name="owned",
    )(pos, total, *halos, *riders, *beside, *after)


def swap(value, r):
    return lax.ppermute(value, "head", [(i, i ^ r) for i in range(4)])


def exchange(value, turn):
    count = lax.axis_size("seq")
    pairs = []
    for s in range(count):
        other = s + 1 if s % 2 == turn else s - 1
        for h in range(4):
            there = other * 4 + h if 0 <= other < count else s * 4 + (h ^ 1)
            pairs.append((s * 4 + h, there))
    return lax.ppermute(value, ("seq", "head"), pairs)


def body(query, key_in, value, grad_out, pattern, live):
    plan = Plan(query.shape[0])
    per, piece = plan.per, plan.piece
    chunks = range(per)
    count = lax.axis_size("seq")
    seq = lax.axis_index("seq")
    met = []
    for turn in range(2):
        other = jnp.where(seq % 2 == turn, seq + 1, seq - 1)
        met.append((other >= 0) & (other < count))
    pos = jnp.stack([seq, lax.axis_index("head"), *met]).astype(jnp.int32)
    table = jnp.concatenate([pattern, live], axis=1).reshape(-1)

    def pick(r, c, out, *at):
        return [(a, ("head", r, c), out, at + (a,)) for a in range(2)]

    every, here, there = list(chunks), [key_in, value], [query, grad_out]

    def for_near(pair, name):
        moves = [m for n, r in enumerate((1, 3)) for c in every for m in pick(r, c, 0, n * per + c)]
        return swap(move(plan, pos, pair, [(2 * per,) + piece], moves, name)[0], 1)

    def for_far(pair, got, group, name, after=()):
        moves = []
        for n, c in enumerate(group):
            moves += pick(2, c, 0, n, 0)
            moves.append((2, (per + c,), 0, (n, 1)))
        shapes = [(len(group), 2) + piece]
        return swap(move(plan, pos, [*pair, got], shapes, moves, name, after=after)[0], 2)

    kv_got = for_near(here, "kv_for_near")
    moves = [m for c in every for m in pick(0, c, 0, c, 0)]
    moves += [(2, (c,), 0, (c, 1)) for c in every]
    own = move(plan, pos, [*here, kv_got], [(per, 2) + piece], moves, "kv_near")[0]
    nears = [own] + [exchange(own, turn) for turn in range(2)]
    kv_parts, qg_parts = [every[:-1], every[-1:]], [every[:1], every[1:]]
    far = [for_far(here, kv_got, kv_parts[0], "kv_for_far", after=[own])]
    qg_got = for_near(there, "qg_for_near")
    qg_fars = [for_far(there, qg_got, qg_parts[0], "qg_for_far", after=far)]
    far.append(for_far(here, kv_got, kv_parts[1], "kv_for_far", after=far))
    qg_fars.append(for_far(there, qg_got, qg_parts[1], "qg_for_far", after=far[1:] + nears[1:]))
    fars = [[m] + [exchange(m, turn) for turn in range(2)] for m in far]

    odq, sums = [], []
    for c in every:
        pair = (2,) + piece
        k, q = int(c not in kv_parts[0]), int(c not in qg_parts[0])
        blocks = [(array, entry(c, *pair)) for array in nears]
        blocks += [(array, entry(c - kv_parts[k][0], *pair)) for array in fars[k]]
        blocks += [(qg_got, entry(c, *piece)), (qg_fars[q], entry(c - qg_parts[q][0], *pair))]
        wait = [odq[0][2][0]] if c == every[-1] else []
        *mine, halo_a, halo_b, total = attend(
            plan, pos, table, c, query, grad_out, blocks, after=wait
        )
        if c < every[-1]:
            mine[2] = [swap(mine[2], 2), 0]
        odq.append(mine)
        halos = [exchange(halo, turn) for turn, halo in enumerate((halo_a, halo_b))]
        sums.append((total, halos))
    dkv, tokens = [], []
    for c in every:
        riders = [odq[-1][2]] if c == 0 else []
        wait = [odq[-2][2][0]] if c == 0 else []
        beside = [dkv[-1][1][0]] if c == every[-1] else []
        first, near, far, token = owned(plan, pos, *sums[c], riders, beside, wait)
        if c < every[-1]:
            far = swap(far, 2)
        if c == 0:
            odq[-1][2] = [far, 0]
        dkv.append([first, near, [far, 2 * len(riders)]])
        tokens.append(token)

    def onward(groups, name, after):
        moves, inputs = [], []
        for n, group in enumerate(groups):
            for c, (_, near, (far, at)) in enumerate(group):
                view = (0,) if near.ndim > len(piece) else ()
                moves += [(len(inputs), view, n, (c, 0)), (len(inputs) + 1, (at + 1,), n, (c, 1))]
                inputs += [near, far]
        shapes = [(len(group), 2) + piece for group in groups]
        return [swap(x, 1) for x in move(plan, pos, inputs, shapes, moves, name, after=after)]

    got = onward([odq[:-1]], "odq_near", [])
    got += onward([odq[-1:], dkv[:1]], "late_near", tokens[1:2])

    shapes = [(plan.tile, HEADS * HEAD_DIM)] * 4
    inputs, moves = list(got), []
    for n, (first, _, (far, at)) in enumerate(odq + dkv[:1]):
        m, c = divmod(n, per)
        source, at_c = (0, n) if n < per - 1 else (n - per + 2, 0)
        pieces = [(len(inputs), ()), (source, (at_c, 0)), (len(inputs) + 1, (at,)), (source, (at_c, 1))]
        for r, (a, view) in enumerate(pieces):
            moves += [(a, view + (b,), 2 * m + b, ("head", r, c)) for b in range(2)]
        inputs += [first, far]
    attended, query_grad, *grads = move(plan, pos, inputs, shapes, moves, "outputs")

    (first_1, _, (far_1, at)), (first_2, near_2, (far_2, _)) = dkv[1:]
    beside = swap(near_2, 1)
    inputs = [first_1, beside, far_1, swap(far_1[at + 1], 1)]
    inputs += [first_2, swap(far_2[0], 2), swap(far_2[1], 3)]
    where = [(0, (), 0, 1), (1, (0,), 1, 1), (2, (at,), 2, 1), (3, (), 3, 1)]
    where += [(4, (), 0, 2), (1, (1,), 1, 2), (5, (), 2, 2), (6, (), 3, 2)]
    moves = [(a, view + (b,), b, ("head", r, c)) for a, view, r, c in where for b in range(2)]
    key_grad, value_grad = move(plan, pos, inputs, shapes[:2], moves, "last", into=grads)
    return attended, query_grad, key_grad, value_grad


def solution(mesh):
    split = P(("groups", "seq", "head"), None)
    return jax.shard_map(
        body,
        mesh=mesh,
        in_specs=(split, split, split, split, P(), P()),
        out_specs=(split, split, split, split),
        check_vma=False,
    )
```
